32 devices in a mesh: tile: 4 (over y, x), head: 8 (over z, core).
Axes of the slice: x: 2, y: 2, z: 4, core: 2. Of those that a mesh axis runs over, the one named last changes fastest.
Arguments:
- embedded: bfloat16 [4, 1024, 16, 16], P('tile', 'head'), may hold values from -6 to 6
- cotangent: bfloat16 [4, 1024, 16, 16], P('tile', 'head'), may hold values from -6 to 6
- weights: bfloat16 [1024, 4, 8, 128], P('head'), may hold values from -0.1875 to 0.1875
Outputs:
- attention: bfloat16 [4, 1024, 16, 16], P('tile', 'head')
- token_grads: float32 [4, 1024, 16, 16], P('tile', 'head')
- weight_grads: float32 [1024, 4, 8, 128], P('head')
The draws below stay inside these ranges and needn't reach their ends.
All inputs are finite; a program needn't handle non-finite values.
Results may differ from the reference program's by a relative error of at most 0.022.
Values may be sent and summed in bfloat16 or wider, within the bound.
A program may use at most 64 MiB of HBM per device.

```python
import jax
import jax.numpy as jnp
from jax import lax

D = 1024
HEADS = 8
HEAD_DIM = 128
TILE_ROWS = 16
TILE_COLS = 16
RIM = 4
TILES_DEV = 1
STRIP = 16
GRID_ROWS = 2
GRID_COLS = 2
PAD_ROWS = 24
PAD_COLS = 24
TILE_TOKENS = 256
PAD_TOKENS = 576
N_TILE = 4


def shard_levels(key, dims, cuts, low, top_value):
    loudness = 1.0
    for axis_at, blocks in cuts:
        steps = jax.random.uniform(jax.random.fold_in(jax.random.fold_in(key, 6), axis_at), (blocks,), jnp.float32, low / len(cuts), top_value / len(cuts))
        loudness = loudness * jnp.repeat(jnp.exp(steps), dims[axis_at] // blocks).reshape((-1,) + (1,) * (len(dims) - 1 - axis_at))
    return loudness


def scatter_about(key, shape, width, bound, split=(), kind=jnp.bfloat16):
    result = jax.random.normal(key, shape, jnp.float32) * width
    if len(split) > 0:
        result = shard_levels(key, shape, split, -0.22, 0.18) * result
    return jnp.clip(result, min=-bound, max=bound).astype(kind)


def setup_inputs(seed: int = 0) -> dict:
    arg_keys = jax.random.split(jax.random.key(seed), 4)
    return {
        "embedded": scatter_about(arg_keys[0], (N_TILE, D, TILE_ROWS, STRIP), 1.0, 6.0, ((0, 4), (1, 8))),
        "cotangent": scatter_about(arg_keys[1], (N_TILE, D, TILE_ROWS, STRIP), 1.0, 6.0, ((0, 4), (1, 8))),
        "weights": scatter_about(arg_keys[2], (D, 4, HEADS, HEAD_DIM), D ** -0.5, 0.1875, ((0, 8),)),
    }


def to_picture(blocks):
    return blocks.reshape(GRID_ROWS, 2, D, TILE_ROWS, STRIP).transpose(0, 3, 1, 4, 2).reshape(GRID_ROWS * TILE_ROWS, 2 * STRIP, D)


def from_picture(picture):
    return picture.reshape(GRID_ROWS, TILE_ROWS, 2, STRIP, D).transpose(0, 2, 4, 1, 3).reshape(GRID_ROWS * 2, D, TILE_ROWS, STRIP)


def reference(embedded, cotangent, weights):
    score_scale = HEAD_DIM ** -0.5
    picture = to_picture(embedded)
    grad_picture = to_picture(cotangent)
    height = GRID_ROWS * TILE_ROWS
    breadth = GRID_COLS * TILE_COLS
    padded = jnp.pad(picture, ((RIM, RIM), (RIM, RIM), (0, 0)))
    wfull = weights.astype(jnp.float32)
    w_query = wfull[:, 0]
    w_key = wfull[:, 1]
    w_value = wfull[:, 2]
    w_out = wfull[:, 3]
    zero_index = jnp.zeros((), jnp.int32)

    def one_tile(state_pair, tile_index):
        grad_field, weight_acc = state_pair
        row_id = tile_index // GRID_COLS
        col_id = tile_index % GRID_COLS
        start_row = (row_id * TILE_ROWS).astype(jnp.int32)
        start_col = (col_id * TILE_COLS).astype(jnp.int32)
        window = lax.dynamic_slice(padded, (start_row, start_col, zero_index), (PAD_ROWS, PAD_COLS, D))
        grad_tile = lax.dynamic_slice(grad_picture, (start_row, start_col, zero_index), (TILE_ROWS, TILE_COLS, D))
        row_pos = start_row + jnp.arange(PAD_ROWS) - RIM
        col_pos = start_col + jnp.arange(PAD_COLS) - RIM
        key_valid = (((row_pos >= 0) & (row_pos < height))[:, None] & ((col_pos >= 0) & (col_pos < breadth))[None, :]).reshape(PAD_TOKENS)
        window_f = window.reshape(PAD_TOKENS, D).astype(jnp.float32)
        inner_f = window[RIM:RIM + TILE_ROWS, RIM:RIM + TILE_COLS].reshape(TILE_TOKENS, D).astype(jnp.float32)
        grad_f = grad_tile.reshape(TILE_TOKENS, D).astype(jnp.float32)
        queries = jnp.einsum('td,dhe->the', inner_f, w_query).astype(jnp.bfloat16).astype(jnp.float32)
        keys = jnp.einsum('pd,dhe->phe', window_f, w_key).astype(jnp.bfloat16).astype(jnp.float32)
        values = jnp.einsum('pd,dhe->phe', window_f, w_value).astype(jnp.bfloat16).astype(jnp.float32)
        scores = jnp.einsum('the,phe->htp', queries, keys) * score_scale
        scores = jnp.where(key_valid[None, None, :], scores, -jnp.inf)
        top_score = jnp.max(scores, axis=-1, keepdims=True)
        expo = jnp.exp(scores - top_score)
        probs = expo / jnp.sum(expo, axis=-1, keepdims=True)
        probs_low = probs.astype(jnp.bfloat16).astype(jnp.float32)
        attended = jnp.einsum('htp,phe->the', probs_low, values).astype(jnp.bfloat16).astype(jnp.float32)
        parts = jnp.einsum('the,dhe->htd', attended, w_out).astype(jnp.bfloat16)
        out_tile = jnp.sum(parts.astype(jnp.float32), axis=0).astype(jnp.bfloat16)
        d_attended = jnp.einsum('td,dhe->the', grad_f, w_out).astype(jnp.bfloat16).astype(jnp.float32)
        grad_out_w = jnp.einsum('td,the->dhe', grad_f, attended)
        d_probs = jnp.einsum('the,phe->htp', d_attended, values)
        d_scores = (probs * (d_probs - jnp.sum(d_probs * probs, axis=-1, keepdims=True)) * score_scale).astype(jnp.bfloat16).astype(jnp.float32)
        d_queries = jnp.einsum('htp,phe->the', d_scores, keys).astype(jnp.bfloat16).astype(jnp.float32)
        d_keys = jnp.einsum('htp,the->phe', d_scores, queries).astype(jnp.bfloat16).astype(jnp.float32)
        d_values = jnp.einsum('htp,the->phe', probs_low, d_attended).astype(jnp.bfloat16).astype(jnp.float32)
        grad_query_w = jnp.einsum('td,the->dhe', inner_f, d_queries)
        grad_key_w = jnp.einsum('pd,phe->dhe', window_f, d_keys)
        grad_value_w = jnp.einsum('pd,phe->dhe', window_f, d_values)
        d_window = jnp.einsum('phe,dhe->hpd', d_keys, w_key) + jnp.einsum('phe,dhe->hpd', d_values, w_value)
        d_inner = jnp.einsum('the,dhe->htd', d_queries, w_query)
        d_window = d_window.reshape(HEADS, PAD_ROWS, PAD_COLS, D).at[:, RIM:RIM + TILE_ROWS, RIM:RIM + TILE_COLS].add(d_inner.reshape(HEADS, TILE_ROWS, TILE_COLS, D))
        d_window = jnp.sum(d_window.astype(jnp.bfloat16).astype(jnp.float32), axis=0)
        current = lax.dynamic_slice(grad_field, (start_row, start_col, zero_index), (PAD_ROWS, PAD_COLS, D))
        grad_field = lax.dynamic_update_slice(grad_field, current + d_window, (start_row, start_col, zero_index))
        weight_term = jnp.stack([grad_query_w, grad_key_w, grad_value_w, grad_out_w], axis=1)
        tile_slot = col_id % TILES_DEV
        weight_acc = weight_acc.at[tile_slot].add(weight_term)
        return (grad_field, weight_acc), out_tile

    grad_start = jnp.zeros((height + 2 * RIM, breadth + 2 * RIM, D), jnp.float32)
    weight_start = jnp.zeros((TILES_DEV, D, 4, HEADS, HEAD_DIM), jnp.float32)
    (grad_field, weight_acc), out_tiles = lax.scan(one_tile, (grad_start, weight_start), jnp.arange(GRID_ROWS * GRID_COLS, dtype=jnp.int32))
    out_picture = out_tiles.reshape(GRID_ROWS, GRID_COLS, TILE_ROWS, TILE_COLS, D).transpose(0, 2, 1, 3, 4).reshape(height, breadth, D)
    attention = from_picture(out_picture)
    token_grads = from_picture(grad_field[RIM:RIM + height, RIM:RIM + breadth])
    rounded = lax.optimization_barrier(weight_acc.astype(jnp.bfloat16))
    weight_grads = jnp.sum(rounded.astype(jnp.float32), axis=0)
    return attention, token_grads, weight_grads
```

```python
import jax
import jax.numpy as jnp
from jax import lax
from jax.experimental import pallas as pl
from jax.experimental.pallas import tpu as pltpu
from jax.sharding import PartitionSpec as P

D = 1024
HEADS = 8
HEAD_DIM = 128
TILE_ROWS = 16
TILE_COLS = 16
RIM = 4
PAD_ROWS = 24
PAD_COLS = 24
TILE_TOKENS = 256
PAD_TOKENS = 576


def passed_along(value, axis, steps):
    count = lax.axis_size(axis)
    leading, last = (max(0, -steps), min(count, count - steps))
    return lax.ppermute(value, axis, [(source, source + steps) for source in range(leading, last)])


def contract(first_op, second_op, first_dim, second_dim):
    return lax.dot_general(
        first_op,
        second_op,
        (((first_dim,), (second_dim,)), ((), ())),
        preferred_element_type=jnp.float32,
    )


def rim_move(piece, shift_by):
    return passed_along(piece.astype(jnp.bfloat16), "tile", shift_by).astype(piece.dtype)


def spread_units(units, per_dev, short_devs):
    if short_devs == 0:
        return units
    head_count = short_devs * (per_dev - 1)
    lead = units[:head_count].reshape((short_devs, per_dev - 1) + units.shape[1:])
    filler = jnp.zeros((short_devs, 1) + units.shape[1:], units.dtype)
    lead = jnp.concatenate([lead, filler], 1).reshape((short_devs * per_dev,) + units.shape[1:])
    return jnp.concatenate([lead, units[head_count:]], 0)


def pack_units(whole, per_dev, short_devs):
    if short_devs == 0:
        return whole
    lead = whole[: short_devs * per_dev].reshape((short_devs, per_dev) + whole.shape[1:])
    lead = lead[:, : per_dev - 1].reshape((short_devs * (per_dev - 1),) + whole.shape[1:])
    return jnp.concatenate([lead, whole[short_devs * per_dev :]], 0)


def local(embedded, cotangent, weights):
    score_scale = HEAD_DIM ** (-0.5)
    n_head = lax.axis_size("head")
    n_tile = lax.axis_size("tile")
    tile_group = n_head // HEADS
    strip_cols = embedded.shape[3]
    width_part = embedded.shape[1]
    tile_id = lax.axis_index("tile")
    head_id = lax.axis_index("head")
    parity = tile_id % 2
    tile_slot = head_id // HEADS
    own_block = embedded[0].astype(jnp.float32)
    from_left = rim_move(own_block[:, :, strip_cols - RIM :], 1)
    from_right = rim_move(own_block[:, :, :RIM], -1)
    from_left = jnp.where(parity == 1, from_left, 0.0)
    from_right = jnp.where(parity == 0, from_right, 0.0)
    widened = jnp.concatenate([from_left, own_block, from_right], 2)
    from_above = rim_move(widened[:, TILE_ROWS - RIM :, :], 2)
    from_below = rim_move(widened[:, :RIM, :], -2)
    padded = jnp.concatenate([from_above, widened, from_below], 1).astype(jnp.bfloat16)
    tile_stack = jnp.stack(
        [
            padded[:, :, member * TILE_COLS : member * TILE_COLS + PAD_COLS]
            for member in range(tile_group)
        ]
    )
    token_send = jnp.repeat(tile_stack.reshape(tile_group, width_part, PAD_TOKENS), HEADS, axis=0)
    grad_tiles = (
        cotangent[0].reshape(width_part, TILE_ROWS, tile_group, TILE_COLS).transpose(2, 0, 1, 3)
    )
    grad_send = jnp.repeat(grad_tiles.reshape(tile_group, width_part, TILE_TOKENS), HEADS, axis=0)
    weight_send = jnp.tile(
        weights.transpose(2, 0, 1, 3).reshape(HEADS, width_part, 4 * HEAD_DIM), (tile_group, 1, 1)
    )
    tokens_in, grads_in, weights_in = (
        lax.all_to_all(token_send, "head", split_axis=0, concat_axis=1, tiled=True),
        lax.all_to_all(grad_send, "head", split_axis=0, concat_axis=1, tiled=True),
        lax.all_to_all(weight_send, "head", split_axis=0, concat_axis=1, tiled=True),
    )
    tokens_all = tokens_in[0]
    grads_all = grads_in[0]
    weight_head = weights_in[0]
    row_pos = tile_id // 2 * TILE_ROWS + jnp.arange(PAD_ROWS) - RIM
    col_pos = (parity * tile_group + tile_slot) * TILE_COLS + jnp.arange(PAD_COLS) - RIM
    height = n_tile // 2 * TILE_ROWS
    breadth = 2 * tile_group * TILE_COLS
    key_valid = (
        ((row_pos >= 0) & (row_pos < height))[:, None]
        & ((col_pos >= 0) & (col_pos < breadth))[None, :]
    ).reshape(PAD_TOKENS)
    interior = tokens_all.reshape(D, PAD_ROWS, PAD_COLS)[
        :, RIM : RIM + TILE_ROWS, RIM : RIM + TILE_COLS
    ].reshape(D, TILE_TOKENS)
    w_query = weight_head[:, :HEAD_DIM]
    w_keyval = weight_head[:, HEAD_DIM : 3 * HEAD_DIM]
    w_out = weight_head[:, 3 * HEAD_DIM :]
    queries = contract(interior, w_query, 0, 0).astype(jnp.bfloat16)
    keyval = contract(tokens_all, w_keyval, 0, 0).astype(jnp.bfloat16)
    keys = keyval[:, :HEAD_DIM]
    values = keyval[:, HEAD_DIM:]
    scores = contract(queries, keys, 1, 1) * score_scale
    scores = jnp.where(key_valid[None, :], scores, -jnp.inf)
    top_score = jnp.max(scores, axis=-1, keepdims=True)
    expo = jnp.exp(scores - top_score)
    probs = expo / jnp.sum(expo, axis=-1, keepdims=True)
    probs_low = probs.astype(jnp.bfloat16)
    attended = jnp.dot(probs_low, values, preferred_element_type=jnp.float32).astype(jnp.bfloat16)
    partial_value = contract(w_out, attended, 1, 1).astype(jnp.bfloat16)
    part_send = partial_value.reshape(n_head, width_part, TILE_TOKENS)
    d_attended = contract(grads_all, w_out, 0, 0).astype(jnp.bfloat16)
    grad_out_w = contract(grads_all, attended, 1, 0)
    d_probs = contract(d_attended, values, 1, 1)
    d_scores = (
        probs * (d_probs - jnp.sum(d_probs * probs, axis=-1, keepdims=True)) * score_scale
    ).astype(jnp.bfloat16)
    d_queries = jnp.dot(d_scores, keys, preferred_element_type=jnp.float32).astype(jnp.bfloat16)
    d_keys = contract(d_scores, queries, 0, 0).astype(jnp.bfloat16)
    d_values = contract(probs_low, d_attended, 0, 0).astype(jnp.bfloat16)
    d_keyval = jnp.concatenate([d_keys, d_values], 1)
    grad_query_w = jnp.dot(interior, d_queries, preferred_element_type=jnp.float32)
    grad_keyval_w = jnp.dot(tokens_all, d_keyval, preferred_element_type=jnp.float32)
    d_tokens = contract(w_keyval, d_keyval, 1, 1)
    d_inner = contract(w_query, d_queries, 1, 1)
    d_tokens = (
        d_tokens.reshape(D, PAD_ROWS, PAD_COLS)
        .at[:, RIM : RIM + TILE_ROWS, RIM : RIM + TILE_COLS]
        .add(d_inner.reshape(D, TILE_ROWS, TILE_COLS))
    )
    d_tokens = d_tokens.reshape(D, PAD_TOKENS).astype(jnp.bfloat16)
    weight_term = jnp.concatenate([grad_query_w, grad_keyval_w, grad_out_w], 1)
    unit_count = 4 * width_part
    unit_dev = (unit_count + n_tile - 1) // n_tile
    short_devs = unit_dev * n_tile - unit_count
    by_unit = weight_term.reshape(n_head, unit_count, HEAD_DIM).transpose(1, 0, 2)
    spread = spread_units(by_unit, unit_dev, short_devs)
    share = lax.psum_scatter(spread.astype(jnp.bfloat16), "tile", scatter_dimension=0, tiled=True)
    weight_send_back = share.transpose(1, 0, 2)
    grad_send_back = d_tokens.reshape(n_head, width_part, PAD_TOKENS)
    parts_back, grads_back, weights_back = (
        lax.all_to_all(part_send, "head", split_axis=0, concat_axis=0, tiled=True),
        lax.all_to_all(grad_send_back, "head", split_axis=0, concat_axis=0, tiled=True),
        lax.all_to_all(weight_send_back, "head", split_axis=0, concat_axis=0, tiled=True),
    )
    out_sum = jnp.sum(
        parts_back.reshape(tile_group, HEADS, width_part, TILE_TOKENS).astype(jnp.float32), axis=1
    ).astype(jnp.bfloat16)
    attention = (
        out_sum.reshape(tile_group, width_part, TILE_ROWS, TILE_COLS)
        .transpose(1, 2, 0, 3)
        .reshape(1, width_part, TILE_ROWS, strip_cols)
    )
    window_grads = jnp.sum(
        grads_back.reshape(tile_group, HEADS, width_part, PAD_TOKENS).astype(jnp.float32), axis=1
    )
    window_grads = window_grads.reshape(tile_group, width_part, PAD_ROWS, PAD_COLS)
    grad_field = jnp.zeros((width_part, PAD_ROWS, strip_cols + 2 * RIM), jnp.float32)
    for member in range(tile_group):
        grad_field = grad_field.at[:, :, member * TILE_COLS : member * TILE_COLS + PAD_COLS].add(
            window_grads[member]
        )
    to_above = rim_move(grad_field[:, :RIM, :], -2)
    to_below = rim_move(grad_field[:, RIM + TILE_ROWS :, :], 2)
    grad_core = grad_field[:, RIM : RIM + TILE_ROWS, :]
    grad_core = grad_core.at[:, TILE_ROWS - RIM :, :].add(to_above).at[:, :RIM, :].add(to_below)
    back_left = rim_move(grad_core[:, :, :RIM], -1)
    back_right = rim_move(grad_core[:, :, RIM + strip_cols :], 1)
    grad_inner = grad_core[:, :, RIM : RIM + strip_cols]
    grad_inner = grad_inner.at[:, :, strip_cols - RIM :].add(jnp.where(parity == 0, back_left, 0.0))
    grad_inner = grad_inner.at[:, :, :RIM].add(jnp.where(parity == 1, back_right, 0.0))
    token_grads = grad_inner[None]
    slot_sum = jnp.sum(
        weights_back.reshape(tile_group, HEADS, unit_dev, HEAD_DIM).astype(jnp.float32), axis=0
    )
    collected = lax.all_gather(slot_sum.transpose(1, 0, 2), "tile", axis=0, tiled=True)
    weight_grads = pack_units(collected, unit_dev, short_devs).reshape(
        width_part, 4, HEADS, HEAD_DIM
    )
    return (attention, token_grads, weight_grads)


BF16 = jnp.bfloat16
F32 = jnp.float32
MESH = pl.DeviceIdType.MESH
SIDE = TILE_ROWS * RIM
FLAT = TILE_COLS * RIM
CORNER = RIM * RIM
RIM_TOKENS = SIDE + FLAT + CORNER
REACH = TILE_TOKENS + RIM_TOKENS
KEY_SLOTS = -(-REACH // 128) * 128


def flip(value, by):
    low, high = by % 2, by // 2
    value_low, value_high = value % 2, value // 2
    value_low = value_low + low - 2 * low * value_low
    value_high = value_high + high - 2 * high * value_high
    return value_low + 2 * value_high


def block(index, size=HEAD_DIM):
    return pl.ds(pl.multiple_of(index * size, size), size)


def rim_choice(tile_id):
    first_row = (TILE_ROWS - RIM) * (1 - tile_id // 2)
    first_col = (TILE_COLS - RIM) * (1 - tile_id % 2)
    row = lax.broadcasted_iota(jnp.int32, (RIM_TOKENS, TILE_TOKENS), 0)
    token = lax.broadcasted_iota(jnp.int32, (RIM_TOKENS, TILE_TOKENS), 1)
    token_row = lax.div(token, jnp.int32(TILE_COLS))
    token_col = lax.rem(token, jnp.int32(TILE_COLS))
    beside = (
        (token_row == lax.div(row, jnp.int32(RIM)))
        & (token_col == first_col + lax.rem(row, jnp.int32(RIM)))
        & (row < SIDE)
    )
    flat = row - SIDE
    above = (token == first_row * TILE_COLS + flat) & (flat >= 0) & (flat < FLAT)
    corner = jnp.maximum(row - SIDE - FLAT, 0)
    across = (
        (token_row == first_row + lax.div(corner, jnp.int32(RIM)))
        & (token_col == first_col + lax.rem(corner, jnp.int32(RIM)))
        & (row >= SIDE + FLAT)
    )
    return jnp.where(beside | above | across, 1.0, 0.0).astype(BF16)


RIM_SPANS = (
    pl.ds(0, SIDE),
    pl.ds(SIDE, FLAT),
    pl.ds(SIDE + FLAT, CORNER),
)
KEY_SPANS = (
    pl.ds(TILE_TOKENS, SIDE),
    pl.ds(TILE_TOKENS + SIDE, FLAT),
    pl.ds(TILE_TOKENS + SIDE + FLAT, CORNER),
)


def fused_kernel(
    xg_ref, w_ref, att_ref, dx_ref, dw_ref,
    xg_all, w_all, kv_send, kv_all, dkv, ret, heads_all, part, got,
    xg_ss, xg_rs, wz_ss, wz_rs, wt_ss, wt_rs, kv_ss, kv_rs, ret_ss, ret_rs,
    hg_ss, hg_rs, rs_ss, rs_rs, ag_ss, ag_rs,
):
    tile_id = lax.axis_index("tile")
    head_id = lax.axis_index("head")
    chip, core = head_id // 2, head_id % 2
    n_tile = 4
    n_chip = HEADS // 2
    share = HEADS * HEAD_DIM // n_tile
    score_scale = HEAD_DIM ** (-0.5)

    def copy(src, dst, send_sem, recv_sem, tile, head):
        return pltpu.make_async_remote_copy(
            src_ref=src, dst_ref=dst, send_sem=send_sem, recv_sem=recv_sem,
            device_id={"tile": tile, "head": head}, device_id_type=MESH,
        )

    def holder(by):
        return 2 * flip(chip, by // 2) + (core + (by % 2) - 2 * (by % 2) * core)

    barrier = pltpu.get_barrier_semaphore()
    for by in range(1, HEADS):
        pl.semaphore_signal(
            barrier, inc=1, device_id={"tile": tile_id, "head": holder(by)}, device_id_type=MESH
        )
    for by in range(1, n_tile):
        pl.semaphore_signal(
            barrier, inc=1, device_id={"tile": flip(tile_id, by), "head": head_id},
            device_id_type=MESH,
        )
    pl.semaphore_wait(barrier, HEADS + n_tile - 2)

    sent = []

    def go(one):
        one.start()
        sent.append(one)
        return one

    class Gather:
        def __init__(self, src, view, ss, rs):
            self.src, self.view, self.ss, self.rs = src, view, ss, rs

        def start(self):
            for by in list(range(2, HEADS, 2)) + [1]:
                self.start_one(by)

        def start_one(self, by):
            go(copy(self.src, self.view(head_id), self.ss.at[by], self.rs.at[by], tile_id, holder(by)))

        def wait(self, by):
            view = self.view(holder(by))
            copy(view, view, self.ss.at[by], self.rs.at[by], tile_id, head_id).wait_recv()

        def pass_on(self, by):
            self.wait(by)
            view = self.view(holder(by))
            go(copy(view, view, self.ss.at[by + 1], self.rs.at[by + 1], tile_id, holder(1)))

        def finish(self):
            for by in range(1, HEADS, 2):
                self.wait(by)

    gathers = [
        Gather(
            xg_ref.at[n],
            lambda holder_id, n=n: xg_all.at[n, :, block(holder_id)],
            xg_ss.at[n], xg_rs.at[n],
        )
        for n in range(2)
    ]
    gathers[0].start()
    for by in range(1, HEADS):
        to = holder(by)
        go(
            copy(
                w_ref.at[tile_id, :, block(to)],
                w_all.at[block(head_id), block(tile_id)],
                wz_ss.at[by], wz_rs.at[by], tile_id, to,
            )
        )
    gathers[1].start()
    for n in range(2):
        xg_all[n, :, block(head_id)] = xg_ref[n]
    w_all[block(head_id), block(tile_id)] = w_ref[tile_id, :, block(head_id)]
    kv_all[REACH:] = jnp.zeros((KEY_SLOTS - REACH, 2 * HEAD_DIM), BF16)
    choice = rim_choice(tile_id)
    x_rows = xg_ref[0].astype(F32).T.astype(BF16)
    g_rows = xg_ref[1].astype(F32).T.astype(BF16)

    two = 2 * HEAD_DIM
    for by_chip in range(n_chip):
        if by_chip > 0:
            gathers[0].pass_on(2 * by_chip)
        for by in (2 * by_chip, 2 * by_chip + 1):
            if by > 0:
                view = w_all.at[block(holder(by)), block(tile_id)]
                copy(view, view, wz_ss.at[by], wz_rs.at[by], tile_id, head_id).wait_recv()
        view = w_all.at[block(flip(chip, by_chip), two), block(tile_id)]
        for by in range(1, n_tile):
            slot = by_chip * n_tile + by
            go(copy(view, view, wt_ss.at[slot], wt_rs.at[slot], flip(tile_id, by), head_id))
    for by_chip in range(1, n_chip):
        gathers[1].pass_on(2 * by_chip)
    gathers[0].finish()
    for by_chip in range(n_chip):
        for by in range(1, n_tile):
            slot = by_chip * n_tile + by
            view = w_all.at[block(flip(chip, by_chip), two), block(flip(tile_id, by))]
            copy(view, view, wt_ss.at[slot], wt_rs.at[slot], tile_id, head_id).wait_recv()

    qkv = jnp.dot(xg_all[0], w_all[:, : 3 * HEAD_DIM], preferred_element_type=F32).astype(BF16)
    queries = qkv[:, :HEAD_DIM]
    own_kv = qkv[:, HEAD_DIM:]
    kv_send[...] = jnp.dot(choice, own_kv, preferred_element_type=F32).astype(BF16)
    for by in range(1, n_tile):
        go(
            copy(
                kv_send.at[RIM_SPANS[by - 1]], kv_all.at[KEY_SPANS[by - 1]],
                kv_ss.at[by], kv_rs.at[by], flip(tile_id, by), head_id,
            )
        )
    gathers[1].finish()
    d_attended = jnp.dot(
        xg_all[1], w_all[:, 3 * HEAD_DIM :], preferred_element_type=F32
    ).astype(BF16)
    for by in range(1, n_tile):
        view = kv_all.at[KEY_SPANS[by - 1]]
        copy(view, view, kv_ss.at[by], kv_rs.at[by], tile_id, head_id).wait_recv()
    rim_kv = kv_all[TILE_TOKENS:]
    keys = jnp.concatenate([own_kv[:, :HEAD_DIM], rim_kv[:, :HEAD_DIM]], 0)
    values = jnp.concatenate([own_kv[:, HEAD_DIM:], rim_kv[:, HEAD_DIM:]], 0)

    scores = contract(queries, keys, 1, 1) * score_scale
    slot_id = lax.broadcasted_iota(jnp.int32, scores.shape, 1)
    scores = jnp.where(slot_id < REACH, scores, -jnp.inf)
    top_score = jnp.max(scores, axis=-1, keepdims=True)
    expo = jnp.exp(scores - top_score)
    probs = expo / jnp.sum(expo, axis=-1, keepdims=True)
    probs_low = probs.astype(BF16)

    head_gathers = [
        Gather(
            heads_all.at[m, :, block(head_id)],
            lambda holder_id, m=m: heads_all.at[m, :, block(holder_id)],
            hg_ss.at[m], hg_rs.at[m],
        )
        for m in range(4)
    ]
    attended = jnp.dot(probs_low, values, preferred_element_type=F32).astype(BF16)
    heads_all[3, :, block(head_id)] = attended
    head_gathers[3].start()
    d_values = contract(probs_low, d_attended, 0, 0)
    d_probs = contract(d_attended, values, 1, 1)
    d_scores = (
        probs * (d_probs - jnp.sum(d_probs * probs, axis=-1, keepdims=True)) * score_scale
    ).astype(BF16)
    d_keys = contract(d_scores, queries, 0, 0)
    d_keyval = jnp.concatenate([d_keys, d_values], 1)
    dkv[...] = d_keyval[TILE_TOKENS:].astype(BF16)
    for by in range(1, n_tile):
        span = RIM_SPANS[by - 1]
        go(copy(dkv.at[span], ret.at[span], ret_ss.at[by], ret_rs.at[by], flip(tile_id, by), head_id))
    heads_all[0, :, block(head_id)] = jnp.dot(
        d_scores, keys, preferred_element_type=F32
    ).astype(BF16)
    head_gathers[0].start()
    for by in range(1, n_tile):
        view = ret.at[RIM_SPANS[by - 1]]
        copy(view, view, ret_ss.at[by], ret_rs.at[by], tile_id, head_id).wait_recv()
    d_keyval = (d_keyval[:TILE_TOKENS] + contract(choice, ret[...], 0, 0)).astype(BF16)
    heads_all[1, :, block(head_id)] = d_keyval[:, :HEAD_DIM]
    heads_all[2, :, block(head_id)] = d_keyval[:, HEAD_DIM:]
    head_gathers[1].start()
    head_gathers[2].start()

    def sum_out(m):
        for by in range(1, n_tile):
            view = got.at[m, by - 1]
            copy(view, view, rs_ss.at[m, by], rs_rs.at[m, by], tile_id, head_id).wait_recv()
        total = part[m, :, block(tile_id, share)].astype(F32)
        for by in range(1, n_tile):
            total = total + got[m, by - 1].astype(F32)
        dw_ref[m, :, block(tile_id, share)] = total.astype(BF16)
        view = dw_ref.at[m, :, block(tile_id, share)]
        for by in range(1, n_tile):
            go(copy(view, view, ag_ss.at[m, by], ag_rs.at[m, by], flip(tile_id, by), head_id))

    d_tokens = None
    order = (3, 0, 1, 2)
    for place, m in enumerate(order):
        for by_chip in range(1, n_chip):
            head_gathers[m].pass_on(2 * by_chip)
        head_gathers[m].finish()
        all_heads = heads_all[m]
        rows = g_rows if m == 3 else x_rows
        part[m] = jnp.dot(rows, all_heads, preferred_element_type=F32).astype(BF16)
        for by in range(1, n_tile):
            to = flip(tile_id, by)
            go(
                copy(
                    part.at[m, :, block(to, share)], got.at[m, by - 1],
                    rs_ss.at[m, by], rs_rs.at[m, by], to, head_id,
                )
            )
        back = contract(w_ref[m], all_heads, 1, 1)
        if m == 3:
            att_ref[...] = back.astype(BF16)
        else:
            d_tokens = back if d_tokens is None else d_tokens + back
        if place > 0:
            sum_out(order[place - 1])
    dx_ref[...] = d_tokens
    sum_out(order[-1])
    for m in order:
        for by in range(1, n_tile):
            view = dw_ref.at[m, :, block(flip(tile_id, by), share)]
            copy(view, view, ag_ss.at[m, by], ag_rs.at[m, by], tile_id, head_id).wait_recv()
    for one in sent:
        one.wait_send()


def local_fused(embedded, cotangent, weights):
    n_tile = lax.axis_size("tile")
    width_part = embedded.shape[1]
    tokens = jnp.concatenate([embedded, cotangent], 0).reshape(2, width_part, TILE_TOKENS)
    tokens = tokens.transpose(0, 2, 1)
    flat_weights = weights.transpose(1, 0, 2, 3).reshape(4, width_part, HEADS * HEAD_DIM)
    vmem = pl.BlockSpec(memory_space=pltpu.VMEM)
    dma = pltpu.SemaphoreType.DMA
    whole = HEADS * HEAD_DIM
    attention, token_grads, weight_grads = pl.pallas_call(
        fused_kernel,
        out_shape=(
            jax.ShapeDtypeStruct((width_part, TILE_TOKENS), BF16),
            jax.ShapeDtypeStruct((width_part, TILE_TOKENS), F32),
            jax.ShapeDtypeStruct((4, width_part, whole), BF16),
        ),
        in_specs=[vmem] * 2,
        out_specs=(vmem,) * 3,
        scratch_shapes=[
            pltpu.VMEM((2, TILE_TOKENS, D), BF16),
            pltpu.VMEM((D, 4 * HEAD_DIM), BF16),
            pltpu.VMEM((RIM_TOKENS, 2 * HEAD_DIM), BF16),
            pltpu.VMEM((KEY_SLOTS, 2 * HEAD_DIM), BF16),
            pltpu.VMEM((KEY_SLOTS - TILE_TOKENS, 2 * HEAD_DIM), BF16),
            pltpu.VMEM((RIM_TOKENS, 2 * HEAD_DIM), BF16),
            pltpu.VMEM((4, TILE_TOKENS, whole), BF16),
            pltpu.VMEM((4, width_part, whole), BF16),
            pltpu.VMEM((4, n_tile - 1, width_part, whole // n_tile), BF16),
            dma((2, HEADS)), dma((2, HEADS)),
            dma((HEADS,)), dma((HEADS,)),
            dma((HEADS // 2 * n_tile,)), dma((HEADS // 2 * n_tile,)),
            dma((n_tile,)), dma((n_tile,)),
            dma((n_tile,)), dma((n_tile,)),
            dma((4, HEADS)), dma((4, HEADS)),
            dma((4, n_tile)), dma((4, n_tile)),
            dma((4, n_tile)), dma((4, n_tile)),
        ],
        compiler_params=pltpu.CompilerParams(
            collective_id=0, has_side_effects=True, vmem_limit_bytes=48 * 2**20
        ),
    )(tokens, flat_weights)
    return (
        attention.reshape(embedded.shape),
        token_grads.reshape(embedded.shape),
        weight_grads.astype(F32).reshape(4, width_part, HEADS, HEAD_DIM).transpose(1, 0, 2, 3),
    )


def solution(mesh):
    one_tile_each = mesh.shape["head"] == HEADS and mesh.shape["tile"] == 2 * 2
    placed = (
        P("tile", "head", None, None),
        P("tile", "head", None, None),
        P("head", None, None, None),
    )
    return jax.shard_map(
        local_fused if one_tile_each else local,
        mesh=mesh,
        in_specs=placed,
        out_specs=(
            P("tile", "head", None, None),
            P("tile", "head", None, None),
            P("head", None, None, None),
        ),
        check_vma=False,
    )
```

```python
import jax
import jax.numpy as jnp
from jax import lax
from jax.experimental import pallas as pl
from jax.experimental.pallas import tpu as pltpu
from jax.sharding import PartitionSpec as P

D = 1024
HEADS = 8
HEAD_DIM = 128
TILE_ROWS = 16
TILE_COLS = 16
RIM = 4
PAD_ROWS = 24
PAD_COLS = 24
TILE_TOKENS = 256
PAD_TOKENS = 576


def passed_along(value, axis, steps):
    count = lax.axis_size(axis)
    leading, last = (max(0, -steps), min(count, count - steps))
    return lax.ppermute(value, axis, [(source, source + steps) for source in range(leading, last)])


def contract(first_op, second_op, first_dim, second_dim):
    return lax.dot_general(
        first_op,
        second_op,
        (((first_dim,), (second_dim,)), ((), ())),
        preferred_element_type=jnp.float32,
    )


def rim_move(piece, shift_by):
    return passed_along(piece.astype(jnp.bfloat16), "tile", shift_by).astype(piece.dtype)


def spread_units(units, per_dev, short_devs):
    if short_devs == 0:
        return units
    head_count = short_devs * (per_dev - 1)
    lead = units[:head_count].reshape((short_devs, per_dev - 1) + units.shape[1:])
    filler = jnp.zeros((short_devs, 1) + units.shape[1:], units.dtype)
    lead = jnp.concatenate([lead, filler], 1).reshape((short_devs * per_dev,) + units.shape[1:])
    return jnp.concatenate([lead, units[head_count:]], 0)


def pack_units(whole, per_dev, short_devs):
    if short_devs == 0:
        return whole
    lead = whole[: short_devs * per_dev].reshape((short_devs, per_dev) + whole.shape[1:])
    lead = lead[:, : per_dev - 1].reshape((short_devs * (per_dev - 1),) + whole.shape[1:])
    return jnp.concatenate([lead, whole[short_devs * per_dev :]], 0)


def local(embedded, cotangent, weights):
    score_scale = HEAD_DIM ** (-0.5)
    n_head = lax.axis_size("head")
    n_tile = lax.axis_size("tile")
    tile_group = n_head // HEADS
    strip_cols = embedded.shape[3]
    width_part = embedded.shape[1]
    tile_id = lax.axis_index("tile")
    head_id = lax.axis_index("head")
    parity = tile_id % 2
    tile_slot = head_id // HEADS
    own_block = embedded[0].astype(jnp.float32)
    from_left = rim_move(own_block[:, :, strip_cols - RIM :], 1)
    from_right = rim_move(own_block[:, :, :RIM], -1)
    from_left = jnp.where(parity == 1, from_left, 0.0)
    from_right = jnp.where(parity == 0, from_right, 0.0)
    widened = jnp.concatenate([from_left, own_block, from_right], 2)
    from_above = rim_move(widened[:, TILE_ROWS - RIM :, :], 2)
    from_below = rim_move(widened[:, :RIM, :], -2)
    padded = jnp.concatenate([from_above, widened, from_below], 1).astype(jnp.bfloat16)
    tile_stack = jnp.stack(
        [
            padded[:, :, member * TILE_COLS : member * TILE_COLS + PAD_COLS]
            for member in range(tile_group)
        ]
    )
    token_send = jnp.repeat(tile_stack.reshape(tile_group, width_part, PAD_TOKENS), HEADS, axis=0)
    grad_tiles = (
        cotangent[0].reshape(width_part, TILE_ROWS, tile_group, TILE_COLS).transpose(2, 0, 1, 3)
    )
    grad_send = jnp.repeat(grad_tiles.reshape(tile_group, width_part, TILE_TOKENS), HEADS, axis=0)
    weight_send = jnp.tile(
        weights.transpose(2, 0, 1, 3).reshape(HEADS, width_part, 4 * HEAD_DIM), (tile_group, 1, 1)
    )
    tokens_in, grads_in, weights_in = (
        lax.all_to_all(token_send, "head", split_axis=0, concat_axis=1, tiled=True),
        lax.all_to_all(grad_send, "head", split_axis=0, concat_axis=1, tiled=True),
        lax.all_to_all(weight_send, "head", split_axis=0, concat_axis=1, tiled=True),
    )
    tokens_all = tokens_in[0]
    grads_all = grads_in[0]
    weight_head = weights_in[0]
    row_pos = tile_id // 2 * TILE_ROWS + jnp.arange(PAD_ROWS) - RIM
    col_pos = (parity * tile_group + tile_slot) * TILE_COLS + jnp.arange(PAD_COLS) - RIM
    height = n_tile // 2 * TILE_ROWS
    breadth = 2 * tile_group * TILE_COLS
    key_valid = (
        ((row_pos >= 0) & (row_pos < height))[:, None]
        & ((col_pos >= 0) & (col_pos < breadth))[None, :]
    ).reshape(PAD_TOKENS)
    interior = tokens_all.reshape(D, PAD_ROWS, PAD_COLS)[
        :, RIM : RIM + TILE_ROWS, RIM : RIM + TILE_COLS
    ].reshape(D, TILE_TOKENS)
    w_query = weight_head[:, :HEAD_DIM]
    w_keyval = weight_head[:, HEAD_DIM : 3 * HEAD_DIM]
    w_out = weight_head[:, 3 * HEAD_DIM :]
    queries = contract(interior, w_query, 0, 0).astype(jnp.bfloat16)
    keyval = contract(tokens_all, w_keyval, 0, 0).astype(jnp.bfloat16)
    keys = keyval[:, :HEAD_DIM]
    values = keyval[:, HEAD_DIM:]
    scores = contract(queries, keys, 1, 1) * score_scale
    scores = jnp.where(key_valid[None, :], scores, -jnp.inf)
    top_score = jnp.max(scores, axis=-1, keepdims=True)
    expo = jnp.exp(scores - top_score)
    probs = expo / jnp.sum(expo, axis=-1, keepdims=True)
    probs_low = probs.astype(jnp.bfloat16)
    attended = jnp.dot(probs_low, values, preferred_element_type=jnp.float32).astype(jnp.bfloat16)
    partial_value = contract(w_out, attended, 1, 1).astype(jnp.bfloat16)
    part_send = partial_value.reshape(n_head, width_part, TILE_TOKENS)
    d_attended = contract(grads_all, w_out, 0, 0).astype(jnp.bfloat16)
    grad_out_w = contract(grads_all, attended, 1, 0)
    d_probs = contract(d_attended, values, 1, 1)
    d_scores = (
        probs * (d_probs - jnp.sum(d_probs * probs, axis=-1, keepdims=True)) * score_scale
    ).astype(jnp.bfloat16)
    d_queries = jnp.dot(d_scores, keys, preferred_element_type=jnp.float32).astype(jnp.bfloat16)
    d_keys = contract(d_scores, queries, 0, 0).astype(jnp.bfloat16)
    d_values = contract(probs_low, d_attended, 0, 0).astype(jnp.bfloat16)
    d_keyval = jnp.concatenate([d_keys, d_values], 1)
    grad_query_w = jnp.dot(interior, d_queries, preferred_element_type=jnp.float32)
    grad_keyval_w = jnp.dot(tokens_all, d_keyval, preferred_element_type=jnp.float32)
    d_tokens = contract(w_keyval, d_keyval, 1, 1)
    d_inner = contract(w_query, d_queries, 1, 1)
    d_tokens = (
        d_tokens.reshape(D, PAD_ROWS, PAD_COLS)
        .at[:, RIM : RIM + TILE_ROWS, RIM : RIM + TILE_COLS]
        .add(d_inner.reshape(D, TILE_ROWS, TILE_COLS))
    )
    d_tokens = d_tokens.reshape(D, PAD_TOKENS).astype(jnp.bfloat16)
    weight_term = jnp.concatenate([grad_query_w, grad_keyval_w, grad_out_w], 1)
    unit_count = 4 * width_part
    unit_dev = (unit_count + n_tile - 1) // n_tile
    short_devs = unit_dev * n_tile - unit_count
    by_unit = weight_term.reshape(n_head, unit_count, HEAD_DIM).transpose(1, 0, 2)
    spread = spread_units(by_unit, unit_dev, short_devs)
    share = lax.psum_scatter(spread.astype(jnp.bfloat16), "tile", scatter_dimension=0, tiled=True)
    weight_send_back = share.transpose(1, 0, 2)
    grad_send_back = d_tokens.reshape(n_head, width_part, PAD_TOKENS)
    parts_back, grads_back, weights_back = (
        lax.all_to_all(part_send, "head", split_axis=0, concat_axis=0, tiled=True),
        lax.all_to_all(grad_send_back, "head", split_axis=0, concat_axis=0, tiled=True),
        lax.all_to_all(weight_send_back, "head", split_axis=0, concat_axis=0, tiled=True),
    )
    out_sum = jnp.sum(
        parts_back.reshape(tile_group, HEADS, width_part, TILE_TOKENS).astype(jnp.float32), axis=1
    ).astype(jnp.bfloat16)
    attention = (
        out_sum.reshape(tile_group, width_part, TILE_ROWS, TILE_COLS)
        .transpose(1, 2, 0, 3)
        .reshape(1, width_part, TILE_ROWS, strip_cols)
    )
    window_grads = jnp.sum(
        grads_back.reshape(tile_group, HEADS, width_part, PAD_TOKENS).astype(jnp.float32), axis=1
    )
    window_grads = window_grads.reshape(tile_group, width_part, PAD_ROWS, PAD_COLS)
    grad_field = jnp.zeros((width_part, PAD_ROWS, strip_cols + 2 * RIM), jnp.float32)
    for member in range(tile_group):
        grad_field = grad_field.at[:, :, member * TILE_COLS : member * TILE_COLS + PAD_COLS].add(
            window_grads[member]
        )
    to_above = rim_move(grad_field[:, :RIM, :], -2)
    to_below = rim_move(grad_field[:, RIM + TILE_ROWS :, :], 2)
    grad_core = grad_field[:, RIM : RIM + TILE_ROWS, :]
    grad_core = grad_core.at[:, TILE_ROWS - RIM :, :].add(to_above).at[:, :RIM, :].add(to_below)
    back_left = rim_move(grad_core[:, :, :RIM], -1)
    back_right = rim_move(grad_core[:, :, RIM + strip_cols :], 1)
    grad_inner = grad_core[:, :, RIM : RIM + strip_cols]
    grad_inner = grad_inner.at[:, :, strip_cols - RIM :].add(jnp.where(parity == 0, back_left, 0.0))
    grad_inner = grad_inner.at[:, :, :RIM].add(jnp.where(parity == 1, back_right, 0.0))
    token_grads = grad_inner[None]
    slot_sum = jnp.sum(
        weights_back.reshape(tile_group, HEADS, unit_dev, HEAD_DIM).astype(jnp.float32), axis=0
    )
    collected = lax.all_gather(slot_sum.transpose(1, 0, 2), "tile", axis=0, tiled=True)
    weight_grads = pack_units(collected, unit_dev, short_devs).reshape(
        width_part, 4, HEADS, HEAD_DIM
    )
    return (attention, token_grads, weight_grads)


BF16 = jnp.bfloat16
F32 = jnp.float32
MESH = pl.DeviceIdType.MESH
SIDE = TILE_ROWS * RIM
FLAT = TILE_COLS * RIM
CORNER = RIM * RIM
RIM_TOKENS = SIDE + FLAT + CORNER
REACH = TILE_TOKENS + RIM_TOKENS
KEY_SLOTS = -(-REACH // 128) * 128


def flip(value, by):
    low, high = by % 2, by // 2
    value_low, value_high = value % 2, value // 2
    value_low = value_low + low - 2 * low * value_low
    value_high = value_high + high - 2 * high * value_high
    return value_low + 2 * value_high


def block(index, size=HEAD_DIM):
    return pl.ds(pl.multiple_of(index * size, size), size)


def rim_choice(tile_id):
    first_row = (TILE_ROWS - RIM) * (1 - tile_id // 2)
    first_col = (TILE_COLS - RIM) * (1 - tile_id % 2)
    row = lax.broadcasted_iota(jnp.int32, (RIM_TOKENS, TILE_TOKENS), 0)
    token = lax.broadcasted_iota(jnp.int32, (RIM_TOKENS, TILE_TOKENS), 1)
    token_row = lax.div(token, jnp.int32(TILE_COLS))
    token_col = lax.rem(token, jnp.int32(TILE_COLS))
    beside = (
        (token_row == lax.div(row, jnp.int32(RIM)))
        & (token_col == first_col + lax.rem(row, jnp.int32(RIM)))
        & (row < SIDE)
    )
    flat = row - SIDE
    above = (token == first_row * TILE_COLS + flat) & (flat >= 0) & (flat < FLAT)
    corner = jnp.maximum(row - SIDE - FLAT, 0)
    across = (
        (token_row == first_row + lax.div(corner, jnp.int32(RIM)))
        & (token_col == first_col + lax.rem(corner, jnp.int32(RIM)))
        & (row >= SIDE + FLAT)
    )
    return jnp.where(beside | above | across, 1.0, 0.0).astype(BF16)


RIM_SPANS = (
    pl.ds(0, SIDE),
    pl.ds(SIDE, FLAT),
    pl.ds(SIDE + FLAT, CORNER),
)
KEY_SPANS = (
    pl.ds(TILE_TOKENS, SIDE),
    pl.ds(TILE_TOKENS + SIDE, FLAT),
    pl.ds(TILE_TOKENS + SIDE + FLAT, CORNER),
)


def fused_kernel(
    xg_ref, w_ref, att_ref, dx_ref, dw_ref,
    xg_all, w_all, kv_send, kv_all, dkv, ret, heads_all, part, got,
    xg_ss, xg_rs, wz_ss, wz_rs, wt_ss, wt_rs, kv_ss, kv_rs, ret_ss, ret_rs,
    hg_ss, hg_rs, rs_ss, rs_rs, ag_ss, ag_rs,
):
    tile_id = lax.axis_index("tile")
    head_id = lax.axis_index("head")
    chip, core = head_id // 2, head_id % 2
    n_tile = 4
    n_chip = HEADS // 2
    share = HEADS * HEAD_DIM // n_tile
    score_scale = HEAD_DIM ** (-0.5)

    def copy(src, dst, send_sem, recv_sem, tile, head):
        return pltpu.make_async_remote_copy(
            src_ref=src, dst_ref=dst, send_sem=send_sem, recv_sem=recv_sem,
            device_id={"tile": tile, "head": head}, device_id_type=MESH,
        )

    def holder(by):
        return 2 * flip(chip, by // 2) + (core + (by % 2) - 2 * (by % 2) * core)

    barrier = pltpu.get_barrier_semaphore()
    for by in range(1, HEADS):
        pl.semaphore_signal(
            barrier, inc=1, device_id={"tile": tile_id, "head": holder(by)}, device_id_type=MESH
        )
    for by in range(1, n_tile):
        pl.semaphore_signal(
            barrier, inc=1, device_id={"tile": flip(tile_id, by), "head": head_id},
            device_id_type=MESH,
        )
    pl.semaphore_wait(barrier, HEADS + n_tile - 2)

    sent = []

    def go(one):
        one.start()
        sent.append(one)
        return one

    class Gather:
        def __init__(self, src, view, ss, rs):
            self.src, self.view, self.ss, self.rs = src, view, ss, rs

        def start(self):
            for by in list(range(2, HEADS, 2)) + [1]:
                self.start_one(by)

        def start_one(self, by):
            go(copy(self.src, self.view(head_id), self.ss.at[by], self.rs.at[by], tile_id, holder(by)))

        def wait(self, by):
            view = self.view(holder(by))
            copy(view, view, self.ss.at[by], self.rs.at[by], tile_id, head_id).wait_recv()

        def pass_on(self, by):
            self.wait(by)
            view = self.view(holder(by))
            go(copy(view, view, self.ss.at[by + 1], self.rs.at[by + 1], tile_id, holder(1)))

        def finish(self):
            for by in range(1, HEADS, 2):
                self.wait(by)

    gathers = [
        Gather(
            xg_ref.at[n],
            lambda holder_id, n=n: xg_all.at[n, :, block(holder_id)],
            xg_ss.at[n], xg_rs.at[n],
        )
        for n in range(2)
    ]
    gathers[0].start()
    for by in range(1, HEADS):
        to = holder(by)
        go(
            copy(
                w_ref.at[tile_id, :, block(to)],
                w_all.at[block(head_id), block(tile_id)],
                wz_ss.at[by], wz_rs.at[by], tile_id, to,
            )
        )
    for n in range(2):
        xg_all[n, :, block(head_id)] = xg_ref[n]
    w_all[block(head_id), block(tile_id)] = w_ref[tile_id, :, block(head_id)]
    kv_all[REACH:] = jnp.zeros((KEY_SLOTS - REACH, 2 * HEAD_DIM), BF16)
    choice = rim_choice(tile_id)
    x_rows = xg_ref[0].astype(F32).T.astype(BF16)
    g_rows = xg_ref[1].astype(F32).T.astype(BF16)

    two = 2 * HEAD_DIM
    for by_chip in range(n_chip):
        if by_chip > 0:
            gathers[0].pass_on(2 * by_chip)
        for by in (2 * by_chip, 2 * by_chip + 1):
            if by > 0:
                view = w_all.at[block(holder(by)), block(tile_id)]
                copy(view, view, wz_ss.at[by], wz_rs.at[by], tile_id, head_id).wait_recv()
        view = w_all.at[block(flip(chip, by_chip), two), block(tile_id)]
        for by in range(1, n_tile):
            slot = by_chip * n_tile + by
            go(copy(view, view, wt_ss.at[slot], wt_rs.at[slot], flip(tile_id, by), head_id))
    gathers[1].start()
    gathers[0].finish()
    for by_chip in range(n_chip):
        for by in range(1, n_tile):
            slot = by_chip * n_tile + by
            view = w_all.at[block(flip(chip, by_chip), two), block(flip(tile_id, by))]
            copy(view, view, wt_ss.at[slot], wt_rs.at[slot], tile_id, head_id).wait_recv()

    qkv = jnp.dot(xg_all[0], w_all[:, : 3 * HEAD_DIM], preferred_element_type=F32).astype(BF16)
    queries = qkv[:, :HEAD_DIM]
    own_kv = qkv[:, HEAD_DIM:]
    kv_send[...] = jnp.dot(choice, own_kv, preferred_element_type=F32).astype(BF16)
    for by in range(1, n_tile):
        go(
            copy(
                kv_send.at[RIM_SPANS[by - 1]], kv_all.at[KEY_SPANS[by - 1]],
                kv_ss.at[by], kv_rs.at[by], flip(tile_id, by), head_id,
            )
        )
    for by_chip in range(1, n_chip):
        gathers[1].pass_on(2 * by_chip)
    for by in range(1, n_tile):
        view = kv_all.at[KEY_SPANS[by - 1]]
        copy(view, view, kv_ss.at[by], kv_rs.at[by], tile_id, head_id).wait_recv()
    rim_kv = kv_all[TILE_TOKENS:]
    keys = jnp.concatenate([own_kv[:, :HEAD_DIM], rim_kv[:, :HEAD_DIM]], 0)
    values = jnp.concatenate([own_kv[:, HEAD_DIM:], rim_kv[:, HEAD_DIM:]], 0)

    scores = contract(queries, keys, 1, 1) * score_scale
    slot_id = lax.broadcasted_iota(jnp.int32, scores.shape, 1)
    scores = jnp.where(slot_id < REACH, scores, -jnp.inf)
    top_score = jnp.max(scores, axis=-1, keepdims=True)
    expo = jnp.exp(scores - top_score)
    probs = expo / jnp.sum(expo, axis=-1, keepdims=True)
    probs_low = probs.astype(BF16)

    head_gathers = [
        Gather(
            heads_all.at[m, :, block(head_id)],
            lambda holder_id, m=m: heads_all.at[m, :, block(holder_id)],
            hg_ss.at[m], hg_rs.at[m],
        )
        for m in range(4)
    ]
    attended = jnp.dot(probs_low, values, preferred_element_type=F32).astype(BF16)
    heads_all[3, :, block(head_id)] = attended
    head_gathers[3].start()
    gathers[1].finish()
    d_attended = jnp.dot(
        xg_all[1], w_all[:, 3 * HEAD_DIM :], preferred_element_type=F32
    ).astype(BF16)
    d_values = contract(probs_low, d_attended, 0, 0)
    d_probs = contract(d_attended, values, 1, 1)
    d_scores = (
        probs * (d_probs - jnp.sum(d_probs * probs, axis=-1, keepdims=True)) * score_scale
    ).astype(BF16)
    d_keys = contract(d_scores, queries, 0, 0)
    d_keyval = jnp.concatenate([d_keys, d_values], 1)
    dkv[...] = d_keyval[TILE_TOKENS:].astype(BF16)
    for by in range(1, n_tile):
        span = RIM_SPANS[by - 1]
        go(copy(dkv.at[span], ret.at[span], ret_ss.at[by], ret_rs.at[by], flip(tile_id, by), head_id))
    heads_all[0, :, block(head_id)] = jnp.dot(
        d_scores, keys, preferred_element_type=F32
    ).astype(BF16)
    head_gathers[0].start()
    for by in range(1, n_tile):
        view = ret.at[RIM_SPANS[by - 1]]
        copy(view, view, ret_ss.at[by], ret_rs.at[by], tile_id, head_id).wait_recv()
    d_keyval = (d_keyval[:TILE_TOKENS] + contract(choice, ret[...], 0, 0)).astype(BF16)
    heads_all[1, :, block(head_id)] = d_keyval[:, :HEAD_DIM]
    heads_all[2, :, block(head_id)] = d_keyval[:, HEAD_DIM:]

    def sum_out(m):
        for by in range(1, n_tile):
            view = got.at[m, by - 1]
            copy(view, view, rs_ss.at[m, by], rs_rs.at[m, by], tile_id, head_id).wait_recv()
        total = part[m, :, block(tile_id, share)].astype(F32)
        for by in range(1, n_tile):
            total = total + got[m, by - 1].astype(F32)
        dw_ref[m, :, block(tile_id, share)] = total.astype(BF16)
        view = dw_ref.at[m, :, block(tile_id, share)]
        for by in range(1, n_tile):
            go(copy(view, view, ag_ss.at[m, by], ag_rs.at[m, by], flip(tile_id, by), head_id))

    d_tokens = None
    order = (3, 0, 1, 2)
    for place, m in enumerate(order):
        for by_chip in range(1, n_chip):
            head_gathers[m].pass_on(2 * by_chip)
        if place + 2 < len(order):
            head_gathers[order[place + 2]].start()
        head_gathers[m].finish()
        all_heads = heads_all[m]
        rows = g_rows if m == 3 else x_rows
        part[m] = jnp.dot(rows, all_heads, preferred_element_type=F32).astype(BF16)
        for by in range(1, n_tile):
            to = flip(tile_id, by)
            go(
                copy(
                    part.at[m, :, block(to, share)], got.at[m, by - 1],
                    rs_ss.at[m, by], rs_rs.at[m, by], to, head_id,
                )
            )
        back = contract(w_ref[m], all_heads, 1, 1)
        if m == 3:
            att_ref[...] = back.astype(BF16)
        else:
            d_tokens = back if d_tokens is None else d_tokens + back
        if place > 0:
            sum_out(order[place - 1])
    dx_ref[...] = d_tokens
    sum_out(order[-1])
    for m in order:
        for by in range(1, n_tile):
            view = dw_ref.at[m, :, block(flip(tile_id, by), share)]
            copy(view, view, ag_ss.at[m, by], ag_rs.at[m, by], tile_id, head_id).wait_recv()
    for one in sent:
        one.wait_send()


def local_fused(embedded, cotangent, weights):
    n_tile = lax.axis_size("tile")
    width_part = embedded.shape[1]
    tokens = jnp.concatenate([embedded, cotangent], 0).reshape(2, width_part, TILE_TOKENS)
    tokens = tokens.transpose(0, 2, 1)
    flat_weights = weights.transpose(1, 0, 2, 3).reshape(4, width_part, HEADS * HEAD_DIM)
    vmem = pl.BlockSpec(memory_space=pltpu.VMEM)
    dma = pltpu.SemaphoreType.DMA
    whole = HEADS * HEAD_DIM
    attention, token_grads, weight_grads = pl.pallas_call(
        fused_kernel,
        out_shape=(
            jax.ShapeDtypeStruct((width_part, TILE_TOKENS), BF16),
            jax.ShapeDtypeStruct((width_part, TILE_TOKENS), F32),
            jax.ShapeDtypeStruct((4, width_part, whole), BF16),
        ),
        in_specs=[vmem] * 2,
        out_specs=(vmem,) * 3,
        scratch_shapes=[
            pltpu.VMEM((2, TILE_TOKENS, D), BF16),
            pltpu.VMEM((D, 4 * HEAD_DIM), BF16),
            pltpu.VMEM((RIM_TOKENS, 2 * HEAD_DIM), BF16),
            pltpu.VMEM((KEY_SLOTS, 2 * HEAD_DIM), BF16),
            pltpu.VMEM((KEY_SLOTS - TILE_TOKENS, 2 * HEAD_DIM), BF16),
            pltpu.VMEM((RIM_TOKENS, 2 * HEAD_DIM), BF16),
            pltpu.VMEM((4, TILE_TOKENS, whole), BF16),
            pltpu.VMEM((4, width_part, whole), BF16),
            pltpu.VMEM((4, n_tile - 1, width_part, whole // n_tile), BF16),
            dma((2, HEADS)), dma((2, HEADS)),
            dma((HEADS,)), dma((HEADS,)),
            dma((HEADS // 2 * n_tile,)), dma((HEADS // 2 * n_tile,)),
            dma((n_tile,)), dma((n_tile,)),
            dma((n_tile,)), dma((n_tile,)),
            dma((4, HEADS)), dma((4, HEADS)),
            dma((4, n_tile)), dma((4, n_tile)),
            dma((4, n_tile)), dma((4, n_tile)),
        ],
        compiler_params=pltpu.CompilerParams(
            collective_id=0, has_side_effects=True, vmem_limit_bytes=48 * 2**20
        ),
    )(tokens, flat_weights)
    return (
        attention.reshape(embedded.shape),
        token_grads.reshape(embedded.shape),
        weight_grads.astype(F32).reshape(4, width_part, HEADS, HEAD_DIM).transpose(1, 0, 2, 3),
    )


def solution(mesh):
    one_tile_each = mesh.shape["head"] == HEADS and mesh.shape["tile"] == 2 * 2
    placed = (
        P("tile", "head", None, None),
        P("tile", "head", None, None),
        P("head", None, None, None),
    )
    return jax.shard_map(
        local_fused if one_tile_each else local,
        mesh=mesh,
        in_specs=placed,
        out_specs=(
            P("tile", "head", None, None),
            P("tile", "head", None, None),
            P("head", None, None, None),
        ),
        check_vma=False,
    )
```

```python
import jax
import jax.numpy as jnp
from jax import lax
from jax.experimental import pallas as pl
from jax.experimental.pallas import tpu as pltpu
from jax.sharding import PartitionSpec as P

D = 1024
HEADS = 8
HEAD_DIM = 128
TILE_ROWS = 16
TILE_COLS = 16
RIM = 4
PAD_ROWS = 24
PAD_COLS = 24
TILE_TOKENS = 256
PAD_TOKENS = 576


def passed_along(value, axis, steps):
    count = lax.axis_size(axis)
    leading, last = (max(0, -steps), min(count, count - steps))
    return lax.ppermute(value, axis, [(source, source + steps) for source in range(leading, last)])


def contract(first_op, second_op, first_dim, second_dim):
    return lax.dot_general(
        first_op,
        second_op,
        (((first_dim,), (second_dim,)), ((), ())),
        preferred_element_type=jnp.float32,
    )


def rim_move(piece, shift_by):
    return passed_along(piece.astype(jnp.bfloat16), "tile", shift_by).astype(piece.dtype)


def spread_units(units, per_dev, short_devs):
    if short_devs == 0:
        return units
    head_count = short_devs * (per_dev - 1)
    lead = units[:head_count].reshape((short_devs, per_dev - 1) + units.shape[1:])
    filler = jnp.zeros((short_devs, 1) + units.shape[1:], units.dtype)
    lead = jnp.concatenate([lead, filler], 1).reshape((short_devs * per_dev,) + units.shape[1:])
    return jnp.concatenate([lead, units[head_count:]], 0)


def pack_units(whole, per_dev, short_devs):
    if short_devs == 0:
        return whole
    lead = whole[: short_devs * per_dev].reshape((short_devs, per_dev) + whole.shape[1:])
    lead = lead[:, : per_dev - 1].reshape((short_devs * (per_dev - 1),) + whole.shape[1:])
    return jnp.concatenate([lead, whole[short_devs * per_dev :]], 0)


def local(embedded, cotangent, weights):
    score_scale = HEAD_DIM ** (-0.5)
    n_head = lax.axis_size("head")
    n_tile = lax.axis_size("tile")
    tile_group = n_head // HEADS
    strip_cols = embedded.shape[3]
    width_part = embedded.shape[1]
    tile_id = lax.axis_index("tile")
    head_id = lax.axis_index("head")
    parity = tile_id % 2
    tile_slot = head_id // HEADS
    own_block = embedded[0].astype(jnp.float32)
    from_left = rim_move(own_block[:, :, strip_cols - RIM :], 1)
    from_right = rim_move(own_block[:, :, :RIM], -1)
    from_left = jnp.where(parity == 1, from_left, 0.0)
    from_right = jnp.where(parity == 0, from_right, 0.0)
    widened = jnp.concatenate([from_left, own_block, from_right], 2)
    from_above = rim_move(widened[:, TILE_ROWS - RIM :, :], 2)
    from_below = rim_move(widened[:, :RIM, :], -2)
    padded = jnp.concatenate([from_above, widened, from_below], 1).astype(jnp.bfloat16)
    tile_stack = jnp.stack(
        [
            padded[:, :, member * TILE_COLS : member * TILE_COLS + PAD_COLS]
            for member in range(tile_group)
        ]
    )
    token_send = jnp.repeat(tile_stack.reshape(tile_group, width_part, PAD_TOKENS), HEADS, axis=0)
    grad_tiles = (
        cotangent[0].reshape(width_part, TILE_ROWS, tile_group, TILE_COLS).transpose(2, 0, 1, 3)
    )
    grad_send = jnp.repeat(grad_tiles.reshape(tile_group, width_part, TILE_TOKENS), HEADS, axis=0)
    weight_send = jnp.tile(
        weights.transpose(2, 0, 1, 3).reshape(HEADS, width_part, 4 * HEAD_DIM), (tile_group, 1, 1)
    )
    tokens_in, grads_in, weights_in = (
        lax.all_to_all(token_send, "head", split_axis=0, concat_axis=1, tiled=True),
        lax.all_to_all(grad_send, "head", split_axis=0, concat_axis=1, tiled=True),
        lax.all_to_all(weight_send, "head", split_axis=0, concat_axis=1, tiled=True),
    )
    tokens_all = tokens_in[0]
    grads_all = grads_in[0]
    weight_head = weights_in[0]
    row_pos = tile_id // 2 * TILE_ROWS + jnp.arange(PAD_ROWS) - RIM
    col_pos = (parity * tile_group + tile_slot) * TILE_COLS + jnp.arange(PAD_COLS) - RIM
    height = n_tile // 2 * TILE_ROWS
    breadth = 2 * tile_group * TILE_COLS
    key_valid = (
        ((row_pos >= 0) & (row_pos < height))[:, None]
        & ((col_pos >= 0) & (col_pos < breadth))[None, :]
    ).reshape(PAD_TOKENS)
    interior = tokens_all.reshape(D, PAD_ROWS, PAD_COLS)[
        :, RIM : RIM + TILE_ROWS, RIM : RIM + TILE_COLS
    ].reshape(D, TILE_TOKENS)
    w_query = weight_head[:, :HEAD_DIM]
    w_keyval = weight_head[:, HEAD_DIM : 3 * HEAD_DIM]
    w_out = weight_head[:, 3 * HEAD_DIM :]
    queries = contract(interior, w_query, 0, 0).astype(jnp.bfloat16)
    keyval = contract(tokens_all, w_keyval, 0, 0).astype(jnp.bfloat16)
    keys = keyval[:, :HEAD_DIM]
    values = keyval[:, HEAD_DIM:]
    scores = contract(queries, keys, 1, 1) * score_scale
    scores = jnp.where(key_valid[None, :], scores, -jnp.inf)
    top_score = jnp.max(scores, axis=-1, keepdims=True)
    expo = jnp.exp(scores - top_score)
    probs = expo / jnp.sum(expo, axis=-1, keepdims=True)
    probs_low = probs.astype(jnp.bfloat16)
    attended = jnp.dot(probs_low, values, preferred_element_type=jnp.float32).astype(jnp.bfloat16)
    partial_value = contract(w_out, attended, 1, 1).astype(jnp.bfloat16)
    part_send = partial_value.reshape(n_head, width_part, TILE_TOKENS)
    d_attended = contract(grads_all, w_out, 0, 0).astype(jnp.bfloat16)
    grad_out_w = contract(grads_all, attended, 1, 0)
    d_probs = contract(d_attended, values, 1, 1)
    d_scores = (
        probs * (d_probs - jnp.sum(d_probs * probs, axis=-1, keepdims=True)) * score_scale
    ).astype(jnp.bfloat16)
    d_queries = jnp.dot(d_scores, keys, preferred_element_type=jnp.float32).astype(jnp.bfloat16)
    d_keys = contract(d_scores, queries, 0, 0).astype(jnp.bfloat16)
    d_values = contract(probs_low, d_attended, 0, 0).astype(jnp.bfloat16)
    d_keyval = jnp.concatenate([d_keys, d_values], 1)
    grad_query_w = jnp.dot(interior, d_queries, preferred_element_type=jnp.float32)
    grad_keyval_w = jnp.dot(tokens_all, d_keyval, preferred_element_type=jnp.float32)
    d_tokens = contract(w_keyval, d_keyval, 1, 1)
    d_inner = contract(w_query, d_queries, 1, 1)
    d_tokens = (
        d_tokens.reshape(D, PAD_ROWS, PAD_COLS)
        .at[:, RIM : RIM + TILE_ROWS, RIM : RIM + TILE_COLS]
        .add(d_inner.reshape(D, TILE_ROWS, TILE_COLS))
    )
    d_tokens = d_tokens.reshape(D, PAD_TOKENS).astype(jnp.bfloat16)
    weight_term = jnp.concatenate([grad_query_w, grad_keyval_w, grad_out_w], 1)
    unit_count = 4 * width_part
    unit_dev = (unit_count + n_tile - 1) // n_tile
    short_devs = unit_dev * n_tile - unit_count
    by_unit = weight_term.reshape(n_head, unit_count, HEAD_DIM).transpose(1, 0, 2)
    spread = spread_units(by_unit, unit_dev, short_devs)
    share = lax.psum_scatter(spread.astype(jnp.bfloat16), "tile", scatter_dimension=0, tiled=True)
    weight_send_back = share.transpose(1, 0, 2)
    grad_send_back = d_tokens.reshape(n_head, width_part, PAD_TOKENS)
    parts_back, grads_back, weights_back = (
        lax.all_to_all(part_send, "head", split_axis=0, concat_axis=0, tiled=True),
        lax.all_to_all(grad_send_back, "head", split_axis=0, concat_axis=0, tiled=True),
        lax.all_to_all(weight_send_back, "head", split_axis=0, concat_axis=0, tiled=True),
    )
    out_sum = jnp.sum(
        parts_back.reshape(tile_group, HEADS, width_part, TILE_TOKENS).astype(jnp.float32), axis=1
    ).astype(jnp.bfloat16)
    attention = (
        out_sum.reshape(tile_group, width_part, TILE_ROWS, TILE_COLS)
        .transpose(1, 2, 0, 3)
        .reshape(1, width_part, TILE_ROWS, strip_cols)
    )
    window_grads = jnp.sum(
        grads_back.reshape(tile_group, HEADS, width_part, PAD_TOKENS).astype(jnp.float32), axis=1
    )
    window_grads = window_grads.reshape(tile_group, width_part, PAD_ROWS, PAD_COLS)
    grad_field = jnp.zeros((width_part, PAD_ROWS, strip_cols + 2 * RIM), jnp.float32)
    for member in range(tile_group):
        grad_field = grad_field.at[:, :, member * TILE_COLS : member * TILE_COLS + PAD_COLS].add(
            window_grads[member]
        )
    to_above = rim_move(grad_field[:, :RIM, :], -2)
    to_below = rim_move(grad_field[:, RIM + TILE_ROWS :, :], 2)
    grad_core = grad_field[:, RIM : RIM + TILE_ROWS, :]
    grad_core = grad_core.at[:, TILE_ROWS - RIM :, :].add(to_above).at[:, :RIM, :].add(to_below)
    back_left = rim_move(grad_core[:, :, :RIM], -1)
    back_right = rim_move(grad_core[:, :, RIM + strip_cols :], 1)
    grad_inner = grad_core[:, :, RIM : RIM + strip_cols]
    grad_inner = grad_inner.at[:, :, strip_cols - RIM :].add(jnp.where(parity == 0, back_left, 0.0))
    grad_inner = grad_inner.at[:, :, :RIM].add(jnp.where(parity == 1, back_right, 0.0))
    token_grads = grad_inner[None]
    slot_sum = jnp.sum(
        weights_back.reshape(tile_group, HEADS, unit_dev, HEAD_DIM).astype(jnp.float32), axis=0
    )
    collected = lax.all_gather(slot_sum.transpose(1, 0, 2), "tile", axis=0, tiled=True)
    weight_grads = pack_units(collected, unit_dev, short_devs).reshape(
        width_part, 4, HEADS, HEAD_DIM
    )
    return (attention, token_grads, weight_grads)


BF16 = jnp.bfloat16
F32 = jnp.float32
MESH = pl.DeviceIdType.MESH
SIDE = TILE_ROWS * RIM
FLAT = TILE_COLS * RIM
CORNER = RIM * RIM
RIM_TOKENS = SIDE + FLAT + CORNER
REACH = TILE_TOKENS + RIM_TOKENS
KEY_SLOTS = -(-REACH // 128) * 128


def flip(value, by):
    low, high = by % 2, by // 2
    value_low, value_high = value % 2, value // 2
    value_low = value_low + low - 2 * low * value_low
    value_high = value_high + high - 2 * high * value_high
    return value_low + 2 * value_high


def block(index, size=HEAD_DIM):
    return pl.ds(pl.multiple_of(index * size, size), size)


def rim_choice(tile_id):
    first_row = (TILE_ROWS - RIM) * (1 - tile_id // 2)
    first_col = (TILE_COLS - RIM) * (1 - tile_id % 2)
    row = lax.broadcasted_iota(jnp.int32, (RIM_TOKENS, TILE_TOKENS), 0)
    token = lax.broadcasted_iota(jnp.int32, (RIM_TOKENS, TILE_TOKENS), 1)
    token_row = lax.div(token, jnp.int32(TILE_COLS))
    token_col = lax.rem(token, jnp.int32(TILE_COLS))
    beside = (
        (token_row == lax.div(row, jnp.int32(RIM)))
        & (token_col == first_col + lax.rem(row, jnp.int32(RIM)))
        & (row < SIDE)
    )
    flat = row - SIDE
    above = (token == first_row * TILE_COLS + flat) & (flat >= 0) & (flat < FLAT)
    corner = jnp.maximum(row - SIDE - FLAT, 0)
    across = (
        (token_row == first_row + lax.div(corner, jnp.int32(RIM)))
        & (token_col == first_col + lax.rem(corner, jnp.int32(RIM)))
        & (row >= SIDE + FLAT)
    )
    return jnp.where(beside | above | across, 1.0, 0.0).astype(BF16)


RIM_SPANS = (
    pl.ds(0, SIDE),
    pl.ds(SIDE, FLAT),
    pl.ds(SIDE + FLAT, CORNER),
)
KEY_SPANS = (
    pl.ds(TILE_TOKENS, SIDE),
    pl.ds(TILE_TOKENS + SIDE, FLAT),
    pl.ds(TILE_TOKENS + SIDE + FLAT, CORNER),
)


def fused_kernel(
    xg_ref, w_ref, att_ref, dx_ref, dw_ref,
    xg_all, w_all, kv_send, kv_all, dkv, ret, heads_all, part, got,
    xg_ss, xg_rs, wz_ss, wz_rs, wt_ss, wt_rs, kv_ss, kv_rs, ret_ss, ret_rs,
    hg_ss, hg_rs, rs_ss, rs_rs, ag_ss, ag_rs,
):
    tile_id = lax.axis_index("tile")
    head_id = lax.axis_index("head")
    chip, core = head_id // 2, head_id % 2
    n_tile = 4
    n_chip = HEADS // 2
    share = HEADS * HEAD_DIM // n_tile
    score_scale = HEAD_DIM ** (-0.5)

    def copy(src, dst, send_sem, recv_sem, tile, head):
        return pltpu.make_async_remote_copy(
            src_ref=src, dst_ref=dst, send_sem=send_sem, recv_sem=recv_sem,
            device_id={"tile": tile, "head": head}, device_id_type=MESH,
        )

    def holder(by):
        return 2 * flip(chip, by // 2) + (core + (by % 2) - 2 * (by % 2) * core)

    barrier = pltpu.get_barrier_semaphore()
    for by in range(1, HEADS):
        pl.semaphore_signal(
            barrier, inc=1, device_id={"tile": tile_id, "head": holder(by)}, device_id_type=MESH
        )
    for by in range(1, n_tile):
        pl.semaphore_signal(
            barrier, inc=1, device_id={"tile": flip(tile_id, by), "head": head_id},
            device_id_type=MESH,
        )
    pl.semaphore_wait(barrier, HEADS + n_tile - 2)

    sent = []

    def go(one):
        one.start()
        sent.append(one)
        return one

    class Gather:
        def __init__(self, src, view, ss, rs):
            self.src, self.view, self.ss, self.rs = src, view, ss, rs

        def start(self):
            for by in list(range(2, HEADS, 2)) + [1]:
                self.start_one(by)

        def start_one(self, by):
            go(copy(self.src, self.view(head_id), self.ss.at[by], self.rs.at[by], tile_id, holder(by)))

        def wait(self, by):
            view = self.view(holder(by))
            copy(view, view, self.ss.at[by], self.rs.at[by], tile_id, head_id).wait_recv()

        def pass_on(self, by):
            self.wait(by)
            view = self.view(holder(by))
            go(copy(view, view, self.ss.at[by + 1], self.rs.at[by + 1], tile_id, holder(1)))

        def finish(self):
            for by in range(1, HEADS, 2):
                self.wait(by)

    gathers = [
        Gather(
            xg_ref.at[n],
            lambda holder_id, n=n: xg_all.at[n, :, block(holder_id)],
            xg_ss.at[n], xg_rs.at[n],
        )
        for n in range(2)
    ]
    gathers[0].start()
    for by in range(1, HEADS):
        to = holder(by)
        go(
            copy(
                w_ref.at[tile_id, :, block(to)],
                w_all.at[block(head_id), block(tile_id)],
                wz_ss.at[by], wz_rs.at[by], tile_id, to,
            )
        )
    for n in range(2):
        xg_all[n, :, block(head_id)] = xg_ref[n]
    w_all[block(head_id), block(tile_id)] = w_ref[tile_id, :, block(head_id)]
    kv_all[REACH:] = jnp.zeros((KEY_SLOTS - REACH, 2 * HEAD_DIM), BF16)
    choice = rim_choice(tile_id)
    x_rows = xg_ref[0].astype(F32).T.astype(BF16)
    g_rows = xg_ref[1].astype(F32).T.astype(BF16)

    two = 2 * HEAD_DIM
    for by_chip in range(n_chip):
        if by_chip > 0:
            gathers[0].pass_on(2 * by_chip)
        for by in (2 * by_chip, 2 * by_chip + 1):
            if by > 0:
                view = w_all.at[block(holder(by)), block(tile_id)]
                copy(view, view, wz_ss.at[by], wz_rs.at[by], tile_id, head_id).wait_recv()
        view = w_all.at[block(flip(chip, by_chip), two), block(tile_id)]
        for by in range(1, n_tile):
            slot = by_chip * n_tile + by
            go(copy(view, view, wt_ss.at[slot], wt_rs.at[slot], flip(tile_id, by), head_id))
    gathers[1].start()
    gathers[0].finish()
    for by_chip in range(n_chip):
        for by in range(1, n_tile):
            slot = by_chip * n_tile + by
            view = w_all.at[block(flip(chip, by_chip), two), block(flip(tile_id, by))]
            copy(view, view, wt_ss.at[slot], wt_rs.at[slot], tile_id, head_id).wait_recv()

    qkv = jnp.dot(xg_all[0], w_all[:, : 3 * HEAD_DIM], preferred_element_type=F32).astype(BF16)
    queries = qkv[:, :HEAD_DIM]
    own_kv = qkv[:, HEAD_DIM:]
    kv_send[...] = jnp.dot(choice, own_kv, preferred_element_type=F32).astype(BF16)
    for by in range(1, n_tile):
        go(
            copy(
                kv_send.at[RIM_SPANS[by - 1]], kv_all.at[KEY_SPANS[by - 1]],
                kv_ss.at[by], kv_rs.at[by], flip(tile_id, by), head_id,
            )
        )
    for by_chip in range(1, n_chip):
        gathers[1].pass_on(2 * by_chip)
    for by in range(1, n_tile):
        view = kv_all.at[KEY_SPANS[by - 1]]
        copy(view, view, kv_ss.at[by], kv_rs.at[by], tile_id, head_id).wait_recv()
    rim_kv = kv_all[TILE_TOKENS:]
    keys = jnp.concatenate([own_kv[:, :HEAD_DIM], rim_kv[:, :HEAD_DIM]], 0)
    values = jnp.concatenate([own_kv[:, HEAD_DIM:], rim_kv[:, HEAD_DIM:]], 0)

    scores = contract(queries, keys, 1, 1) * score_scale
    slot_id = lax.broadcasted_iota(jnp.int32, scores.shape, 1)
    scores = jnp.where(slot_id < REACH, scores, -jnp.inf)
    top_score = jnp.max(scores, axis=-1, keepdims=True)
    expo = jnp.exp(scores - top_score)
    probs = expo / jnp.sum(expo, axis=-1, keepdims=True)
    probs_low = probs.astype(BF16)

    head_gathers = [
        Gather(
            heads_all.at[m, :, block(head_id)],
            lambda holder_id, m=m: heads_all.at[m, :, block(holder_id)],
            hg_ss.at[m], hg_rs.at[m],
        )
        for m in range(4)
    ]
    attended = jnp.dot(probs_low, values, preferred_element_type=F32).astype(BF16)
    heads_all[3, :, block(head_id)] = attended
    head_gathers[3].start()
    gathers[1].finish()
    d_attended = jnp.dot(
        xg_all[1], w_all[:, 3 * HEAD_DIM :], preferred_element_type=F32
    ).astype(BF16)
    d_values = contract(probs_low, d_attended, 0, 0)
    d_probs = contract(d_attended, values, 1, 1)
    d_scores = (
        probs * (d_probs - jnp.sum(d_probs * probs, axis=-1, keepdims=True)) * score_scale
    ).astype(BF16)
    d_keys = contract(d_scores, queries, 0, 0)
    d_keyval = jnp.concatenate([d_keys, d_values], 1)
    dkv[...] = d_keyval[TILE_TOKENS:].astype(BF16)
    for by in range(1, n_tile):
        span = RIM_SPANS[by - 1]
        go(copy(dkv.at[span], ret.at[span], ret_ss.at[by], ret_rs.at[by], flip(tile_id, by), head_id))
    heads_all[0, :, block(head_id)] = jnp.dot(
        d_scores, keys, preferred_element_type=F32
    ).astype(BF16)
    head_gathers[0].start()
    for by in range(1, n_tile):
        view = ret.at[RIM_SPANS[by - 1]]
        copy(view, view, ret_ss.at[by], ret_rs.at[by], tile_id, head_id).wait_recv()
    d_keyval = (d_keyval[:TILE_TOKENS] + contract(choice, ret[...], 0, 0)).astype(BF16)
    heads_all[1, :, block(head_id)] = d_keyval[:, :HEAD_DIM]
    heads_all[2, :, block(head_id)] = d_keyval[:, HEAD_DIM:]

    def sum_out(m):
        for by in range(1, n_tile):
            view = got.at[m, by - 1]
            copy(view, view, rs_ss.at[m, by], rs_rs.at[m, by], tile_id, head_id).wait_recv()
        total = part[m, :, block(tile_id, share)].astype(F32)
        for by in range(1, n_tile):
            total = total + got[m, by - 1].astype(F32)
        dw_ref[m, :, block(tile_id, share)] = total.astype(BF16)
        view = dw_ref.at[m, :, block(tile_id, share)]
        for by in range(1, n_tile):
            go(copy(view, view, ag_ss.at[m, by], ag_rs.at[m, by], flip(tile_id, by), head_id))

    d_tokens = None
    order = (3, 0, 1, 2)
    for place, m in enumerate(order):
        for by_chip in range(1, n_chip):
            head_gathers[m].pass_on(2 * by_chip)
            if place > 0 and by_chip == 2:
                sum_out(order[place - 1])
        if place + 2 < len(order):
            head_gathers[order[place + 2]].start()
        head_gathers[m].finish()
        all_heads = heads_all[m]
        rows = g_rows if m == 3 else x_rows
        part[m] = jnp.dot(rows, all_heads, preferred_element_type=F32).astype(BF16)
        for by in range(1, n_tile):
            to = flip(tile_id, by)
            go(
                copy(
                    part.at[m, :, block(to, share)], got.at[m, by - 1],
                    rs_ss.at[m, by], rs_rs.at[m, by], to, head_id,
                )
            )
        back = contract(w_ref[m], all_heads, 1, 1)
        if m == 3:
            att_ref[...] = back.astype(BF16)
        else:
            d_tokens = back if d_tokens is None else d_tokens + back
    dx_ref[...] = d_tokens
    sum_out(order[-1])
    for m in order:
        for by in range(1, n_tile):
            view = dw_ref.at[m, :, block(flip(tile_id, by), share)]
            copy(view, view, ag_ss.at[m, by], ag_rs.at[m, by], tile_id, head_id).wait_recv()
    for one in sent:
        one.wait_send()


def local_fused(embedded, cotangent, weights):
    n_tile = lax.axis_size("tile")
    width_part = embedded.shape[1]
    tokens = jnp.concatenate([embedded, cotangent], 0).reshape(2, width_part, TILE_TOKENS)
    tokens = tokens.transpose(0, 2, 1)
    flat_weights = weights.transpose(1, 0, 2, 3).reshape(4, width_part, HEADS * HEAD_DIM)
    vmem = pl.BlockSpec(memory_space=pltpu.VMEM)
    dma = pltpu.SemaphoreType.DMA
    whole = HEADS * HEAD_DIM
    attention, token_grads, weight_grads = pl.pallas_call(
        fused_kernel,
        out_shape=(
            jax.ShapeDtypeStruct((width_part, TILE_TOKENS), BF16),
            jax.ShapeDtypeStruct((width_part, TILE_TOKENS), F32),
            jax.ShapeDtypeStruct((4, width_part, whole), BF16),
        ),
        in_specs=[vmem] * 2,
        out_specs=(vmem,) * 3,
        scratch_shapes=[
            pltpu.VMEM((2, TILE_TOKENS, D), BF16),
            pltpu.VMEM((D, 4 * HEAD_DIM), BF16),
            pltpu.VMEM((RIM_TOKENS, 2 * HEAD_DIM), BF16),
            pltpu.VMEM((KEY_SLOTS, 2 * HEAD_DIM), BF16),
            pltpu.VMEM((KEY_SLOTS - TILE_TOKENS, 2 * HEAD_DIM), BF16),
            pltpu.VMEM((RIM_TOKENS, 2 * HEAD_DIM), BF16),
            pltpu.VMEM((4, TILE_TOKENS, whole), BF16),
            pltpu.VMEM((4, width_part, whole), BF16),
            pltpu.VMEM((4, n_tile - 1, width_part, whole // n_tile), BF16),
            dma((2, HEADS)), dma((2, HEADS)),
            dma((HEADS,)), dma((HEADS,)),
            dma((HEADS // 2 * n_tile,)), dma((HEADS // 2 * n_tile,)),
            dma((n_tile,)), dma((n_tile,)),
            dma((n_tile,)), dma((n_tile,)),
            dma((4, HEADS)), dma((4, HEADS)),
            dma((4, n_tile)), dma((4, n_tile)),
            dma((4, n_tile)), dma((4, n_tile)),
        ],
        compiler_params=pltpu.CompilerParams(
            collective_id=0, has_side_effects=True, vmem_limit_bytes=48 * 2**20
        ),
    )(tokens, flat_weights)
    return (
        attention.reshape(embedded.shape),
        token_grads.reshape(embedded.shape),
        weight_grads.astype(F32).reshape(4, width_part, HEADS, HEAD_DIM).transpose(1, 0, 2, 3),
    )


def solution(mesh):
    one_tile_each = mesh.shape["head"] == HEADS and mesh.shape["tile"] == 2 * 2
    placed = (
        P("tile", "head", None, None),
        P("tile", "head", None, None),
        P("head", None, None, None),
    )
    return jax.shard_map(
        local_fused if one_tile_each else local,
        mesh=mesh,
        in_specs=placed,
        out_specs=(
            P("tile", "head", None, None),
            P("tile", "head", None, None),
            P("head", None, None, None),
        ),
        check_vma=False,
    )
```
